512 devices in a mesh: seq: 16 (over x, z_hi), head: 8 (over y), dp: 4 (over z_lo, core).
Axes of the slice: x: 4, y: 8, z: 8 (z_hi: 4, z_lo: 2; z = z_hi * 2 + z_lo), core: 2. Of those that a mesh axis runs over, the one named last changes fastest.
Arguments:
- queries: bfloat16 [32768, 4096], P(('dp', 'seq'), 'head'), parts along dimension 0, may hold values from -6 to 6
- key_vectors: bfloat16 [32768, 4096], P(('dp', 'seq'), 'head'), parts along dimension 0, may hold values from -6 to 6
- value_vectors: bfloat16 [32768, 4096], P(('dp', 'seq'), 'head'), parts along dimension 0, may hold values from -13 to 13
- norm_gain: float32 [4096], P('head'), may hold values from 0.1 to 1.9
- cotangent: bfloat16 [32768, 4096], P(('dp', 'seq'), 'head'), parts along dimension 0, may hold values from -6 to 6
Outputs:
- layer_out: bfloat16 [32768, 4096], P(('dp', 'seq'), 'head'), parts along dimension 0
- grad_query: bfloat16 [32768, 4096], P(('dp', 'seq'), 'head'), parts along dimension 0
- grad_key: bfloat16 [32768, 4096], P(('dp', 'seq'), 'head'), parts along dimension 0
- grad_value: bfloat16 [32768, 4096], P(('dp', 'seq'), 'head'), parts along dimension 0
The draws below stay inside these ranges and needn't reach their ends.
There are 4 independent parts, one for each index of `dp`. The reference program is written for one: setup_inputs(seed, part) draws one part's arguments, and reference() takes and returns one part's arrays. A program takes and returns all parts, laid end to end along the dimension named above; an argument that names none is the same for every part. Nothing has to cross between parts.
All inputs are finite; a program needn't handle non-finite values.
Results may differ from the reference program's by a relative error of at most 0.0058.
Values sent between devices are 32-bit elements; how exact they have to be, the bound alone decides.
No kernel may reach another device: no remote copies, remote signals or barrier semaphores. Data moves between devices by JAX's collectives and lax.ppermute only.
A program may use at most 64 MiB of HBM per device.

```python
import jax
import jax.numpy as jnp
from jax import lax

HD = 128
HEADS = 32
BLOCK = 512
TOKENS = 8192
FEAT = 4096


def draw_value_vectors(key, part):
    key = jax.random.fold_in(key, 11)
    subkeys = jax.random.split(key, 3)
    row_scale = 10.0 ** (0.5 * jax.random.uniform(subkeys[0], (TOKENS, 1)))
    position = (jnp.arange(HEADS * HD) // HD).astype(jnp.float32) / max(HEADS - 1, 1)
    spread = jax.random.uniform(subkeys[1], (HEADS * HD,))
    col_scale = 10.0 ** (0.5 * position + 0.5 * spread)
    noise = jnp.clip(jax.random.normal(subkeys[2], (TOKENS, HEADS * HD)), -4.0, 4.0)
    return (0.1 * noise * row_scale * col_scale).astype(jnp.bfloat16)


def block_levels(rng, extent, cuts, smallest, high):
    factor_of, own = 1.0, jax.random.fold_in(rng, 6)
    for axis_at, parts in cuts:
        draws = jnp.exp(jax.random.uniform(jax.random.fold_in(own, axis_at), (parts,), jnp.float32, smallest / len(cuts), high / len(cuts)))
        factor_of = factor_of * jnp.repeat(draws, extent[axis_at] // parts).reshape([-1 if axis == axis_at else 1 for axis in range(len(extent))])
    return factor_of


def bell_draw(stream_key, extent, scale, limit, pieces=(), held_as=jnp.bfloat16):
    array = scale * jax.random.normal(stream_key, extent, jnp.float32)
    if pieces:
        array = array * block_levels(stream_key, extent, pieces, -0.22, 0.18)
    return jnp.clip(array, -limit, limit).astype(held_as)


def setup_inputs(seed: int = 0, part: int = 0) -> dict:
    key_list = jax.random.split(jax.random.key(seed), 6)
    part_keys = jax.random.split(jax.random.fold_in(key_list[5], part), 6)
    return {
        "queries": bell_draw(part_keys[0], (TOKENS, FEAT), 1.0, 6.0, ((0, 16), (1, 8))),
        "key_vectors": bell_draw(part_keys[1], (TOKENS, FEAT), 1.0, 6.0, ((0, 16), (1, 8))),
        "value_vectors": draw_value_vectors(jax.random.fold_in(jax.random.fold_in(key_list[5], part), 71), part),
        "norm_gain": jnp.clip(1.0 + 0.18 * jax.random.normal(key_list[3], (FEAT,), jnp.float32), 0.1, 1.9),
        "cotangent": bell_draw(part_keys[4], (TOKENS, FEAT), 1.0, 6.0, ((0, 16), (1, 8))),
    }


EPS = 1e-06

def to_low(values_in):
    return lax.optimization_barrier(values_in.astype(jnp.bfloat16)).astype(jnp.float32)

def reference(queries, key_vectors, value_vectors, norm_gain, cotangent):
    highest = lax.Precision.HIGHEST
    block_count = TOKENS // BLOCK
    block_shape = (block_count, BLOCK, HEADS, HD)
    query_blocks = queries.astype(jnp.float32).reshape(block_shape)
    key_blocks = key_vectors.astype(jnp.float32).reshape(block_shape)
    value_blocks = value_vectors.astype(jnp.float32).reshape(block_shape)
    positions = jnp.arange(BLOCK)
    causal = positions[:, None] >= positions[None, :]

    def forward_step(prefix_state, blocks):
        query_b, key_b, value_b = blocks
        prefix_low = to_low(prefix_state)
        scores = jnp.einsum('thd,shd->hts', query_b, key_b, precision=highest)
        block_weights = to_low(jnp.where(causal, scores, 0.0))
        attended = jnp.einsum('thd,hde->the', query_b, prefix_low, precision=highest)
        attended = attended + jnp.einsum('hts,she->the', block_weights, value_b, precision=highest)
        local_kv = jnp.einsum('shd,she->hde', key_b, value_b, precision=highest)
        return (prefix_state + local_kv, (attended, prefix_state))
    start_state = jnp.zeros((HEADS, HD, HD), jnp.float32)
    _, (attended_blocks, prefix_states) = lax.scan(forward_step, start_state, (query_blocks, key_blocks, value_blocks))
    attended = attended_blocks.reshape(TOKENS, FEAT)
    inverse_rms = lax.rsqrt(lax.optimization_barrier(jnp.sum(attended * attended, axis=1)) / FEAT + EPS)[:, None]
    layer_out = (attended * inverse_rms * norm_gain).astype(jnp.bfloat16)
    scaled_grad = cotangent.astype(jnp.float32) * norm_gain
    inner = lax.optimization_barrier(jnp.sum(scaled_grad * attended, axis=1))[:, None]
    out_grad = to_low(inverse_rms * (scaled_grad - attended * inner * inverse_rms * inverse_rms / FEAT))
    grad_blocks = out_grad.reshape(block_shape)

    def backward_step(suffix_state, blocks):
        query_b, key_b, value_b, grad_b, prefix_state = blocks
        suffix_low = to_low(suffix_state)
        prefix_low = to_low(prefix_state)
        scores = jnp.einsum('thd,shd->hts', query_b, key_b, precision=highest)
        block_weights = to_low(jnp.where(causal, scores, 0.0))
        grad_scores = jnp.einsum('the,she->hts', grad_b, value_b, precision=highest)
        grad_weights = to_low(jnp.where(causal, grad_scores, 0.0))
        query_grad = jnp.einsum('the,hde->thd', grad_b, prefix_low, precision=highest)
        query_grad = query_grad + jnp.einsum('hts,shd->thd', grad_weights, key_b, precision=highest)
        key_grad = jnp.einsum('she,hde->shd', value_b, suffix_low, precision=highest)
        key_grad = key_grad + jnp.einsum('hts,thd->shd', grad_weights, query_b, precision=highest)
        value_grad = jnp.einsum('shd,hde->she', key_b, suffix_low, precision=highest)
        value_grad = value_grad + jnp.einsum('hts,the->she', block_weights, grad_b, precision=highest)
        local_qg = jnp.einsum('thd,the->hde', query_b, grad_b, precision=highest)
        return (suffix_state + local_qg, (query_grad, key_grad, value_grad))
    _, (query_grads, key_grads, value_grads) = lax.scan(backward_step, start_state, (query_blocks, key_blocks, value_blocks, grad_blocks, prefix_states), reverse=True)
    grad_query = query_grads.reshape(TOKENS, FEAT).astype(jnp.bfloat16)
    grad_key = key_grads.reshape(TOKENS, FEAT).astype(jnp.bfloat16)
    grad_value = value_grads.reshape(TOKENS, FEAT).astype(jnp.bfloat16)
    return (layer_out, grad_query, grad_key, grad_value)
```

```python
import jax
import jax.numpy as jnp
from jax import lax
from jax.experimental import pallas as pl
from jax.experimental.pallas import tpu as pltpu
from jax.sharding import PartitionSpec as P

HD = 128
FEAT = 4096
EPS = 1e-06
F32 = jnp.float32
BF16 = jnp.bfloat16
VMEM_LIMIT = 24 * 1024 * 1024


def dot(a, b, contract):
    return lax.dot_general(a, b, ((contract[0], contract[1]), ((), ())), preferred_element_type=F32)


def nn(a, b):
    return dot(a, b, ((1,), (0,)))


def nt(a, b):
    return dot(a, b, ((1,), (1,)))


def tn(a, b):
    return dot(a, b, ((0,), (0,)))


def head_columns(h):
    return slice(h * HD, (h + 1) * HD)


def call(kernel, out_shape, flops, bytes_accessed, *operands):
    return pl.pallas_call(
        kernel,
        out_shape=out_shape,
        compiler_params=pltpu.CompilerParams(vmem_limit_bytes=VMEM_LIMIT),
        cost_estimate=pl.CostEstimate(
            flops=flops, bytes_accessed=bytes_accessed, transcendentals=0
        ),
    )(*operands)


def shape_of(shape, dtype=F32):
    return jax.ShapeDtypeStruct(shape, dtype)


def state_of_heads(ref, heads):
    return ref[...].reshape(heads, HD, HD)


def outer_kernel(heads, a_ref, b_ref, state_ref):
    per_head = state_ref.shape[0] // heads
    rows = state_ref.shape[1]
    for h in range(heads):
        cols = head_columns(h)
        state = tn(a_ref[:, cols], b_ref[:, cols])
        state_ref[h * per_head : (h + 1) * per_head] = state.reshape(per_head, rows, HD)


def prefix_kernel(part_ref, out_ref):
    n = part_ref.shape[0]
    total = jnp.zeros(part_ref.shape[1:], F32)
    for m in range(n):
        out_ref[m] = total
        if m < n - 1:
            total = total + part_ref[m]


def suffix_kernel(part_ref, out_ref):
    n = part_ref.shape[0]
    total = jnp.zeros(part_ref.shape[1:], F32)
    for m in reversed(range(n)):
        out_ref[m] = total
        if m > 0:
            total = total + part_ref[m]


def masked(block):
    t = lax.broadcasted_iota(jnp.int32, block.shape, 0)
    s = lax.broadcasted_iota(jnp.int32, block.shape, 1)
    return jnp.where(t >= s, block, 0.0).astype(BF16)


def local_kernel(heads, q_ref, k_ref, v_ref, w_ref, l_ref):
    for h in range(heads):
        cols = head_columns(h)
        weights = masked(nt(q_ref[:, cols], k_ref[:, cols]))
        w_ref[h] = weights
        l_ref[:, cols] = nn(weights, v_ref[:, cols])


def attend_kernel(heads, q_ref, p_ref, l_ref, c_ref, g_ref, a_ref, sums_ref):
    state = state_of_heads(p_ref, heads).astype(BF16)
    squares = jnp.zeros((q_ref.shape[0], HD), F32)
    inner = jnp.zeros((q_ref.shape[0], HD), F32)
    for h in range(heads):
        cols = head_columns(h)
        attended = nn(q_ref[:, cols], state[h]) + l_ref[:, cols]
        a_ref[:, cols] = attended
        scaled = c_ref[:, cols].astype(F32) * g_ref[:, cols]
        squares = squares + attended * attended
        inner = inner + scaled * attended
    squares = jnp.sum(squares.T, axis=0, keepdims=True)
    inner = jnp.sum(inner.T, axis=0, keepdims=True)
    both = jnp.concatenate([squares, inner], axis=0)
    for i in range(sums_ref.shape[0]):
        sums_ref[i] = both


def norm_kernel(heads, s_ref, a_ref, c_ref, g_ref, q_ref, o_ref, d_ref, state_ref):
    sums = s_ref[0]
    for i in range(1, s_ref.shape[0]):
        sums = sums + s_ref[i]
    inverse = lax.rsqrt(sums[0:1] / FEAT + EPS)
    slope = sums[1:2] * inverse * inverse / FEAT
    rows = jnp.concatenate(
        [jnp.broadcast_to(inverse, (64, inverse.shape[1])), jnp.broadcast_to(slope, (64, slope.shape[1]))],
        axis=0,
    ).T
    inverse = rows[:, 0:1]
    slope = rows[:, 64:65]
    per_head = state_ref.shape[0] // heads
    for h in range(heads):
        cols = head_columns(h)
        attended = a_ref[:, cols]
        gain = g_ref[:, cols]
        scaled = c_ref[:, cols].astype(F32) * gain
        grad = (inverse * (scaled - attended * slope)).astype(BF16)
        d_ref[:, cols] = grad
        o_ref[:, cols] = (attended * inverse * gain).astype(BF16)
        state = tn(q_ref[:, cols], grad)
        state_ref[h * per_head : (h + 1) * per_head] = state.reshape(
            per_head, state_ref.shape[1], HD
        )


def grad_kernel(heads, d_ref, q_ref, k_ref, v_ref, w_ref, p_ref, gq_ref, gk_ref, gv_ref):
    state = state_of_heads(p_ref, heads).astype(BF16)
    for h in range(heads):
        cols = head_columns(h)
        grad = d_ref[:, cols]
        weights = masked(nt(grad, v_ref[:, cols]))
        gq_ref[:, cols] = (nt(grad, state[h]) + nn(weights, k_ref[:, cols])).astype(BF16)
        gk_ref[:, cols] = tn(weights, q_ref[:, cols])
        gv_ref[:, cols] = tn(w_ref[h], grad)


def final_kernel(heads, s_ref, k_ref, v_ref, gk_ref, gv_ref, key_ref, value_ref):
    state = state_of_heads(s_ref, heads).astype(BF16)
    for h in range(heads):
        cols = head_columns(h)
        key_ref[:, cols] = (nt(v_ref[:, cols], state[h]) + gk_ref[:, cols]).astype(BF16)
        value_ref[:, cols] = (nn(k_ref[:, cols], state[h]) + gv_ref[:, cols]).astype(BF16)


def exchange(parts, axis):
    return lax.all_to_all(parts, axis, 0, 0, tiled=True)


def per_device(queries, key_vectors, value_vectors, norm_gain, cotangent):
    tokens, features = queries.shape
    heads = features // HD
    seq = lax.axis_size("seq")
    head_devices = lax.axis_size("head")
    state_shape = (seq, heads * HD // seq, HD)
    wide = (tokens, features)
    gain = norm_gain.reshape(1, features)

    def bind(kernel):
        return lambda *refs: kernel(heads, *refs)

    product = 2 * tokens * features * HD
    square = 2 * tokens * tokens * features
    size = tokens * features

    with jax.named_scope("key_value_state"):
        local_kv = call(
            bind(outer_kernel), shape_of(state_shape), product, 5 * size, key_vectors, value_vectors
        )
    with jax.named_scope("prefix"):
        pieces = exchange(local_kv, "seq")
        sums = call(prefix_kernel, shape_of(state_shape), 0, size, pieces)
        prefix = exchange(sums, "seq")
    with jax.named_scope("inside_block"):
        weights, local = call(
            bind(local_kernel),
            (shape_of((heads, tokens, tokens), BF16), shape_of(wide)),
            2 * square,
            10 * size,
            queries,
            key_vectors,
            value_vectors,
        )
    with jax.named_scope("attended"):
        attended, sums = call(
            bind(attend_kernel),
            (shape_of(wide), shape_of((head_devices, 2, tokens))),
            product,
            12 * size,
            queries,
            prefix,
            local,
            cotangent,
            gain,
        )
        sums = exchange(sums, "head")
    with jax.named_scope("norm"):
        layer_out, out_grad, local_qg = call(
            bind(norm_kernel),
            (shape_of(wide, BF16), shape_of(wide, BF16), shape_of(state_shape)),
            product,
            12 * size,
            sums,
            attended,
            cotangent,
            gain,
            queries,
        )
    with jax.named_scope("suffix"):
        pieces = exchange(local_qg, "seq")
        sums = call(suffix_kernel, shape_of(state_shape), 0, size, pieces)
        suffix = exchange(sums, "seq")
    with jax.named_scope("grad_parts"):
        grad_query, key_part, value_part = call(
            bind(grad_kernel),
            (shape_of(wide, BF16), shape_of(wide), shape_of(wide)),
            4 * square,
            20 * size,
            out_grad,
            queries,
            key_vectors,
            value_vectors,
            weights,
            prefix,
        )
    with jax.named_scope("grads"):
        grad_key, grad_value = call(
            bind(final_kernel),
            (shape_of(wide, BF16), shape_of(wide, BF16)),
            2 * product,
            16 * size,
            suffix,
            key_vectors,
            value_vectors,
            key_part,
            value_part,
        )
    return (layer_out, grad_query, grad_key, grad_value)


def solution(mesh):
    split = P(("dp", "seq"), "head")
    return jax.shard_map(
        per_device,
        mesh=mesh,
        in_specs=(split, split, split, P("head"), split),
        out_specs=(split, split, split, split),
        check_vma=False,
    )
```

```python
import jax
import jax.numpy as jnp
from jax import lax
from jax.experimental import pallas as pl
from jax.experimental.pallas import tpu as pltpu
from jax.sharding import PartitionSpec as P

HD = 128
FEAT = 4096
EPS = 1e-06
F32 = jnp.float32
BF16 = jnp.bfloat16
VMEM_LIMIT = 24 * 1024 * 1024


def dot(a, b, contract):
    return lax.dot_general(a, b, ((contract[0], contract[1]), ((), ())), preferred_element_type=F32)


def nn(a, b):
    return dot(a, b, ((1,), (0,)))


def nt(a, b):
    return dot(a, b, ((1,), (1,)))


def tn(a, b):
    return dot(a, b, ((0,), (0,)))


def head_columns(h):
    return slice(h * HD, (h + 1) * HD)


def call(kernel, out_shape, *operands, **extra):
    return pl.pallas_call(
        kernel,
        out_shape=out_shape,
        compiler_params=pltpu.CompilerParams(vmem_limit_bytes=VMEM_LIMIT),
        **extra,
    )(*operands)


def shape_of(shape, dtype=F32):
    return jax.ShapeDtypeStruct(shape, dtype)


def state_of_heads(ref, heads):
    return ref[...].reshape(heads, HD, HD).astype(BF16)


def store_state(state_ref, heads, h, state):
    per_head = state_ref.shape[0] // heads
    state_ref[h * per_head : (h + 1) * per_head] = state.reshape(per_head, state_ref.shape[1], HD)


def outer_kernel(heads, a_hbm, b_hbm, state_ref, a_ref, b_ref, sems):
    copies = []
    parts = halves(a_ref.shape[0])
    for j, rows in enumerate(parts):
        pair = []
        for i, (source, target) in enumerate(((a_hbm, a_ref), (b_hbm, b_ref))):
            copy = pltpu.make_async_copy(source.at[rows], target.at[rows], sems.at[j, i])
            copy.start()
            pair.append(copy)
        copies.append(pair)
    states = [None] * heads
    for j, rows in enumerate(parts):
        for copy in copies[j]:
            copy.wait()
        for h in range(heads):
            cols = head_columns(h)
            state = tn(a_ref[rows, cols], b_ref[rows, cols])
            states[h] = state if j == 0 else states[h] + state
    for h in range(heads):
        store_state(state_ref, heads, h, states[h])


def prefix_kernel(part_ref, out_ref):
    n = part_ref.shape[0]
    total = jnp.zeros(part_ref.shape[1:], F32)
    for m in range(n):
        out_ref[m] = total
        if m < n - 1:
            total = total + part_ref[m]


def suffix_kernel(part_ref, out_ref):
    n = part_ref.shape[0]
    total = jnp.zeros(part_ref.shape[1:], F32)
    for m in reversed(range(n)):
        out_ref[m] = total
        if m > 0:
            total = total + part_ref[m]


def causal_mask(rows):
    t = lax.broadcasted_iota(jnp.int32, (rows, rows), 0)
    s = lax.broadcasted_iota(jnp.int32, (rows, rows), 1)
    return t >= s


def cut(block, mask):
    return jnp.where(mask, block, 0.0).astype(BF16)


def halves(tokens):
    return slice(0, tokens // 2), slice(tokens // 2, tokens)


def attend_kernel(heads, q_ref, k_ref, v_ref, p_ref, c_ref, g_ref, a_ref, w_ref, sums_ref):
    tokens = q_ref.shape[0]
    state = state_of_heads(p_ref, heads)
    mask = causal_mask(tokens // 2)
    first, second = halves(tokens)
    squares = [jnp.zeros((tokens // 2, HD), F32)] * 2
    inner = [jnp.zeros((tokens // 2, HD), F32)] * 2
    for h in range(heads):
        cols = head_columns(h)
        q0, q1 = q_ref[first, cols], q_ref[second, cols]
        k0, k1 = k_ref[first, cols], k_ref[second, cols]
        v0, v1 = v_ref[first, cols], v_ref[second, cols]
        w00 = cut(nt(q0, k0), mask)
        w10 = nt(q1, k0).astype(BF16)
        w11 = cut(nt(q1, k1), mask)
        w_ref[h, 0] = w00
        w_ref[h, 1] = w10
        w_ref[h, 2] = w11
        attended = (
            nn(q0, state[h]) + nn(w00, v0),
            nn(q1, state[h]) + (nn(w10, v0) + nn(w11, v1)),
        )
        for i, rows in enumerate((first, second)):
            a_ref[rows, cols] = attended[i]
            scaled = c_ref[rows, cols].astype(F32) * g_ref[:, cols]
            squares[i] = squares[i] + attended[i] * attended[i]
            inner[i] = inner[i] + scaled * attended[i]
    squares = jnp.concatenate([jnp.sum(part.T, axis=0, keepdims=True) for part in squares], axis=1)
    inner = jnp.concatenate([jnp.sum(part.T, axis=0, keepdims=True) for part in inner], axis=1)
    both = jnp.concatenate([squares, inner], axis=0)
    for i in range(sums_ref.shape[0]):
        sums_ref[i] = both


def norm_columns(s_ref):
    sums = s_ref[0]
    for i in range(1, s_ref.shape[0]):
        sums = sums + s_ref[i]
    inverse = lax.rsqrt(sums[0:1] / FEAT + EPS)
    slope = sums[1:2] * inverse * inverse / FEAT
    tokens = sums.shape[1]
    rows = jnp.concatenate(
        [jnp.broadcast_to(inverse, (64, tokens)), jnp.broadcast_to(slope, (64, tokens))], axis=0
    ).T
    return rows[:, 0:1], rows[:, 64:65]


def norm_kernel(heads, s_ref, a_ref, c_ref, g_ref, q_ref, d_ref, state_ref):
    inverse, slope = norm_columns(s_ref)
    for h in range(heads):
        cols = head_columns(h)
        scaled = c_ref[:, cols].astype(F32) * g_ref[:, cols]
        grad = (inverse * (scaled - a_ref[:, cols] * slope)).astype(BF16)
        d_ref[:, cols] = grad
        store_state(state_ref, heads, h, tn(q_ref[:, cols], grad))


def grad_kernel(
    heads, r_ref, s_ref, a_ref, g_ref, d_ref, q_ref, k_ref, v_ref, w_ref, p_ref,
    o_hbm, gq_hbm, gk_hbm, gv_hbm, o_ref, gq_ref, gk_ref, gv_ref, sems,
):
    copies = []

    def send(i, h, source, target):
        cols = head_columns(h)
        copy = pltpu.make_async_copy(source.at[:, cols], target.at[:, cols], sems.at[i, h])
        copy.start()
        copies.append(copy)

    tokens = q_ref.shape[0]
    first, second = halves(tokens)
    mask = causal_mask(tokens // 2)
    inverse, _ = norm_columns(s_ref)
    for h in range(heads):
        cols = head_columns(h)
        o_ref[:, cols] = (a_ref[:, cols] * inverse * g_ref[:, cols]).astype(BF16)
        send(0, h, o_ref, o_hbm)
    prefix = state_of_heads(p_ref, heads)
    suffix = state_of_heads(r_ref, heads)
    for h in range(heads):
        cols = head_columns(h)
        q0, q1 = q_ref[first, cols], q_ref[second, cols]
        k0, k1 = k_ref[first, cols], k_ref[second, cols]
        v0, v1 = v_ref[first, cols], v_ref[second, cols]
        d0, d1 = d_ref[first, cols], d_ref[second, cols]
        g00 = cut(nt(d0, v0), mask)
        g10 = nt(d1, v0).astype(BF16)
        g11 = cut(nt(d1, v1), mask)
        gq_ref[first, cols] = (nt(d0, prefix[h]) + nn(g00, k0)).astype(BF16)
        gq_ref[second, cols] = (nt(d1, prefix[h]) + (nn(g10, k0) + nn(g11, k1))).astype(BF16)
        send(1, h, gq_ref, gq_hbm)
        gk_ref[first, cols] = (nt(v0, suffix[h]) + (tn(g00, q0) + tn(g10, q1))).astype(BF16)
        gk_ref[second, cols] = (nt(v1, suffix[h]) + tn(g11, q1)).astype(BF16)
        send(2, h, gk_ref, gk_hbm)
        w00, w10, w11 = w_ref[h, 0], w_ref[h, 1], w_ref[h, 2]
        gv_ref[first, cols] = (nn(k0, suffix[h]) + (tn(w00, d0) + tn(w10, d1))).astype(BF16)
        gv_ref[second, cols] = (nn(k1, suffix[h]) + tn(w11, d1)).astype(BF16)
        send(3, h, gv_ref, gv_hbm)
    for copy in copies:
        copy.wait()


def exchange(parts, axis):
    return lax.all_to_all(parts, axis, 0, 0, tiled=True)


def per_device(queries, key_vectors, value_vectors, norm_gain, cotangent):
    tokens, features = queries.shape
    heads = features // HD
    seq = lax.axis_size("seq")
    head_devices = lax.axis_size("head")
    state_shape = (seq, heads * HD // seq, HD)
    wide = (tokens, features)
    gain = norm_gain.reshape(1, features)

    def bind(kernel):
        return lambda *refs: kernel(heads, *refs)

    in_hbm = pl.BlockSpec(memory_space=pltpu.HBM)
    in_vmem = pl.BlockSpec(memory_space=pltpu.VMEM)

    with jax.named_scope("key_value_state"):
        local_kv = call(
            bind(outer_kernel),
            shape_of(state_shape),
            pltpu.with_memory_space_constraint(key_vectors, pltpu.HBM),
            pltpu.with_memory_space_constraint(value_vectors, pltpu.HBM),
            in_specs=[in_hbm, in_hbm],
            out_specs=in_vmem,
            scratch_shapes=[
                pltpu.VMEM(wide, BF16),
                pltpu.VMEM(wide, BF16),
                pltpu.SemaphoreType.DMA((heads, 2)),
            ],
        )
    with jax.named_scope("prefix"):
        pieces = exchange(local_kv, "seq")
        sums = call(prefix_kernel, shape_of(state_shape), pieces)
        prefix = exchange(sums, "seq")
    with jax.named_scope("attended"):
        attended, weights, sums = call(
            bind(attend_kernel),
            (
                shape_of(wide),
                shape_of((heads, 3, tokens // 2, tokens // 2), BF16),
                shape_of((head_devices, 2, tokens)),
            ),
            queries,
            key_vectors,
            value_vectors,
            prefix,
            cotangent,
            gain,
        )
        sums = exchange(sums, "head")
    with jax.named_scope("norm"):
        out_grad, local_qg = call(
            bind(norm_kernel),
            (shape_of(wide, BF16), shape_of(state_shape)),
            sums,
            attended,
            cotangent,
            gain,
            queries,
        )
    with jax.named_scope("suffix"):
        pieces = exchange(local_qg, "seq")
        totals = call(suffix_kernel, shape_of(state_shape), pieces)
        suffix = exchange(totals, "seq")
    with jax.named_scope("grads"):
        return call(
            bind(grad_kernel),
            (shape_of(wide, BF16),) * 4,
            suffix,
            sums,
            attended,
            gain,
            out_grad,
            queries,
            key_vectors,
            value_vectors,
            weights,
            prefix,
            in_specs=[in_vmem] * 10,
            out_specs=[in_hbm] * 4,
            scratch_shapes=[pltpu.VMEM(wide, BF16)] * 4 + [pltpu.SemaphoreType.DMA((4, heads))],
        )


def solution(mesh):
    split = P(("dp", "seq"), "head")
    return jax.shard_map(
        per_device,
        mesh=mesh,
        in_specs=(split, split, split, P("head"), split),
        out_specs=(split, split, split, split),
        check_vma=False,
    )
```

```python
import jax
import jax.numpy as jnp
from jax import lax
from jax.experimental import pallas as pl
from jax.experimental.pallas import tpu as pltpu
from jax.sharding import PartitionSpec as P

HD = 128
FEAT = 4096
EPS = 1e-06
F32 = jnp.float32
BF16 = jnp.bfloat16
VMEM_LIMIT = 24 * 1024 * 1024


def dot(a, b, contract):
    return lax.dot_general(a, b, ((contract[0], contract[1]), ((), ())), preferred_element_type=F32)


def nn(a, b):
    return dot(a, b, ((1,), (0,)))


def nt(a, b):
    return dot(a, b, ((1,), (1,)))


def tn(a, b):
    return dot(a, b, ((0,), (0,)))


def head_columns(h):
    return slice(h * HD, (h + 1) * HD)


def call(kernel, out_shape, *operands, **extra):
    return pl.pallas_call(
        kernel,
        out_shape=out_shape,
        compiler_params=pltpu.CompilerParams(vmem_limit_bytes=VMEM_LIMIT),
        **extra,
    )(*operands)


def shape_of(shape, dtype=F32):
    return jax.ShapeDtypeStruct(shape, dtype)


def state_of_heads(ref, heads):
    return ref[...].reshape(heads, HD, HD).astype(BF16)


def store_state(state_ref, heads, h, state):
    per_head = state_ref.shape[0] // heads
    state_ref[h * per_head : (h + 1) * per_head] = state.reshape(per_head, state_ref.shape[1], HD)


def outer_kernel(heads, a_hbm, b_hbm, state_ref, a_ref, b_ref, sems):
    copies = []
    parts = halves(a_ref.shape[0])
    for j, rows in enumerate(parts):
        pair = []
        for i, (source, target) in enumerate(((a_hbm, a_ref), (b_hbm, b_ref))):
            copy = pltpu.make_async_copy(source.at[rows], target.at[rows], sems.at[j, i])
            copy.start()
            pair.append(copy)
        copies.append(pair)
    states = [None] * heads
    for j, rows in enumerate(parts):
        for copy in copies[j]:
            copy.wait()
        for h in range(heads):
            cols = head_columns(h)
            state = tn(a_ref[rows, cols], b_ref[rows, cols])
            states[h] = state if j == 0 else states[h] + state
    for h in range(heads):
        store_state(state_ref, heads, h, states[h])


def prefix_kernel(part_ref, out_ref):
    n = part_ref.shape[0]
    total = jnp.zeros(part_ref.shape[1:], F32)
    for m in range(n):
        out_ref[m] = total
        if m < n - 1:
            total = total + part_ref[m]


def suffix_kernel(part_ref, out_ref):
    n = part_ref.shape[0]
    total = jnp.zeros(part_ref.shape[1:], F32)
    for m in reversed(range(n)):
        out_ref[m] = total
        if m > 0:
            total = total + part_ref[m]


def causal_mask(rows):
    t = lax.broadcasted_iota(jnp.int32, (rows, rows), 0)
    s = lax.broadcasted_iota(jnp.int32, (rows, rows), 1)
    return t >= s


def cut(block, mask):
    return jnp.where(mask, block, 0.0).astype(BF16)


def halves(tokens):
    return slice(0, tokens // 2), slice(tokens // 2, tokens)


def attend_kernel(heads, q_ref, k_ref, v_ref, p_ref, c_ref, g_ref, a_ref, w_ref, sums_ref):
    tokens = q_ref.shape[0]
    state = state_of_heads(p_ref, heads)
    mask = causal_mask(tokens // 2)
    first, second = halves(tokens)
    squares = [jnp.zeros((tokens // 2, HD), F32)] * 2
    inner = [jnp.zeros((tokens // 2, HD), F32)] * 2
    for h in range(heads):
        cols = head_columns(h)
        q0, q1 = q_ref[first, cols], q_ref[second, cols]
        k0, k1 = k_ref[first, cols], k_ref[second, cols]
        w00 = cut(nt(q0, k0), mask)
        w10 = nt(q1, k0).astype(BF16)
        w11 = cut(nt(q1, k1), mask)
        w_ref[h, 0] = w00
        w_ref[h, 1] = w10
        w_ref[h, 2] = w11
    for h in range(heads):
        cols = head_columns(h)
        q0, q1 = q_ref[first, cols], q_ref[second, cols]
        v0, v1 = v_ref[first, cols], v_ref[second, cols]
        w00, w10, w11 = w_ref[h, 0], w_ref[h, 1], w_ref[h, 2]
        attended = (
            nn(q0, state[h]) + nn(w00, v0),
            nn(q1, state[h]) + (nn(w10, v0) + nn(w11, v1)),
        )
        for i, rows in enumerate((first, second)):
            a_ref[rows, cols] = attended[i]
    for h in range(heads):
        cols = head_columns(h)
        for i, rows in enumerate((first, second)):
            part = a_ref[rows, cols]
            scaled = c_ref[rows, cols].astype(F32) * g_ref[:, cols]
            squares[i] = squares[i] + part * part
            inner[i] = inner[i] + scaled * part
    squares = jnp.concatenate([jnp.sum(part.T, axis=0, keepdims=True) for part in squares], axis=1)
    inner = jnp.concatenate([jnp.sum(part.T, axis=0, keepdims=True) for part in inner], axis=1)
    both = jnp.concatenate([squares, inner], axis=0)
    for i in range(sums_ref.shape[0]):
        sums_ref[i] = both


def norm_columns(s_ref):
    sums = s_ref[0]
    for i in range(1, s_ref.shape[0]):
        sums = sums + s_ref[i]
    inverse = lax.rsqrt(sums[0:1] / FEAT + EPS)
    slope = sums[1:2] * inverse * inverse / FEAT
    tokens = sums.shape[1]
    rows = jnp.concatenate(
        [jnp.broadcast_to(inverse, (64, tokens)), jnp.broadcast_to(slope, (64, tokens))], axis=0
    ).T
    return rows[:, 0:1], rows[:, 64:65]


def norm_kernel(heads, s_ref, a_ref, c_ref, g_ref, q_ref, d_ref, state_ref, o_ref):
    inverse, slope = norm_columns(s_ref)
    for h in range(heads):
        cols = head_columns(h)
        scaled = c_ref[:, cols].astype(F32) * g_ref[:, cols]
        grad = (inverse * (scaled - a_ref[:, cols] * slope)).astype(BF16)
        d_ref[:, cols] = grad
        store_state(state_ref, heads, h, tn(q_ref[:, cols], grad))
        o_ref[:, cols] = (a_ref[:, cols] * inverse * g_ref[:, cols]).astype(BF16)


def grad_kernel(
    heads, r_ref, d_ref, q_ref, k_ref, v_ref, w_ref, p_ref, o_ref,
    o_hbm, gq_hbm, gk_hbm, gv_hbm, gq_ref, gk_ref, gv_ref, gw_ref, sems,
):
    copies = []

    def send(i, h, source, target):
        cols = head_columns(h)
        copy = pltpu.make_async_copy(source.at[:, cols], target.at[:, cols], sems.at[i, h])
        copy.start()
        copies.append(copy)

    for h in range(heads):
        send(0, h, o_ref, o_hbm)
    tokens = q_ref.shape[0]
    first, second = halves(tokens)
    mask = causal_mask(tokens // 2)
    prefix = state_of_heads(p_ref, heads)
    suffix = state_of_heads(r_ref, heads)
    for h in range(heads):
        cols = head_columns(h)
        v0, v1 = v_ref[first, cols], v_ref[second, cols]
        d0, d1 = d_ref[first, cols], d_ref[second, cols]
        gw_ref[h, 0] = cut(nt(d0, v0), mask)
        gw_ref[h, 1] = nt(d1, v0).astype(BF16)
        gw_ref[h, 2] = cut(nt(d1, v1), mask)
    for h in range(heads):
        cols = head_columns(h)
        q0, q1 = q_ref[first, cols], q_ref[second, cols]
        k0, k1 = k_ref[first, cols], k_ref[second, cols]
        v0, v1 = v_ref[first, cols], v_ref[second, cols]
        d0, d1 = d_ref[first, cols], d_ref[second, cols]
        g00, g10, g11 = gw_ref[h, 0], gw_ref[h, 1], gw_ref[h, 2]
        gq_ref[first, cols] = (nt(d0, prefix[h]) + nn(g00, k0)).astype(BF16)
        gq_ref[second, cols] = (nt(d1, prefix[h]) + (nn(g10, k0) + nn(g11, k1))).astype(BF16)
        send(1, h, gq_ref, gq_hbm)
        gk_ref[first, cols] = (nt(v0, suffix[h]) + (tn(g00, q0) + tn(g10, q1))).astype(BF16)
        gk_ref[second, cols] = (nt(v1, suffix[h]) + tn(g11, q1)).astype(BF16)
        send(2, h, gk_ref, gk_hbm)
        w00, w10, w11 = w_ref[h, 0], w_ref[h, 1], w_ref[h, 2]
        gv_ref[first, cols] = (nn(k0, suffix[h]) + (tn(w00, d0) + tn(w10, d1))).astype(BF16)
        gv_ref[second, cols] = (nn(k1, suffix[h]) + tn(w11, d1)).astype(BF16)
        send(3, h, gv_ref, gv_hbm)
    for copy in copies:
        copy.wait()


def exchange(parts, axis):
    return lax.all_to_all(parts, axis, 0, 0, tiled=True)


def per_device(queries, key_vectors, value_vectors, norm_gain, cotangent):
    tokens, features = queries.shape
    heads = features // HD
    seq = lax.axis_size("seq")
    head_devices = lax.axis_size("head")
    state_shape = (seq, heads * HD // seq, HD)
    wide = (tokens, features)
    gain = norm_gain.reshape(1, features)

    def bind(kernel):
        return lambda *refs: kernel(heads, *refs)

    in_hbm = pl.BlockSpec(memory_space=pltpu.HBM)
    in_vmem = pl.BlockSpec(memory_space=pltpu.VMEM)

    with jax.named_scope("key_value_state"):
        local_kv = call(
            bind(outer_kernel),
            shape_of(state_shape),
            pltpu.with_memory_space_constraint(key_vectors, pltpu.HBM),
            pltpu.with_memory_space_constraint(value_vectors, pltpu.HBM),
            in_specs=[in_hbm, in_hbm],
            out_specs=in_vmem,
            scratch_shapes=[
                pltpu.VMEM(wide, BF16),
                pltpu.VMEM(wide, BF16),
                pltpu.SemaphoreType.DMA((heads, 2)),
            ],
        )
    with jax.named_scope("prefix"):
        pieces = exchange(local_kv, "seq")
        sums = call(prefix_kernel, shape_of(state_shape), pieces)
        prefix = exchange(sums, "seq")
    with jax.named_scope("attended"):
        attended, weights, sums = call(
            bind(attend_kernel),
            (
                shape_of(wide),
                shape_of((heads, 3, tokens // 2, tokens // 2), BF16),
                shape_of((head_devices, 2, tokens)),
            ),
            queries,
            key_vectors,
            value_vectors,
            prefix,
            cotangent,
            gain,
        )
        sums = exchange(sums, "head")
    with jax.named_scope("norm"):
        out_grad, local_qg, layer_out = call(
            bind(norm_kernel),
            (shape_of(wide, BF16), shape_of(state_shape), shape_of(wide, BF16)),
            sums,
            attended,
            cotangent,
            gain,
            queries,
        )
    with jax.named_scope("suffix"):
        pieces = exchange(local_qg, "seq")
        totals = call(suffix_kernel, shape_of(state_shape), pieces)
        suffix = exchange(totals, "seq")
    with jax.named_scope("grads"):
        return call(
            bind(grad_kernel),
            (shape_of(wide, BF16),) * 4,
            suffix,
            out_grad,
            queries,
            key_vectors,
            value_vectors,
            weights,
            prefix,
            layer_out,
            in_specs=[in_vmem] * 8,
            out_specs=[in_hbm] * 4,
            scratch_shapes=[pltpu.VMEM(wide, BF16)] * 3 + [pltpu.VMEM((heads, 3, tokens // 2, tokens // 2), BF16), pltpu.SemaphoreType.DMA((4, heads))],
        )


def solution(mesh):
    split = P(("dp", "seq"), "head")
    return jax.shard_map(
        per_device,
        mesh=mesh,
        in_specs=(split, split, split, P("head"), split),
        out_specs=(split, split, split, split),
        check_vma=False,
    )
```

```python
import functools

import jax
import jax.numpy as jnp
from jax import lax
from jax.experimental import pallas as pl
from jax.experimental.pallas import tpu as pltpu
from jax.sharding import PartitionSpec as P

HD = 128
FEAT = 4096
EPS = 1e-06
F32 = jnp.float32
BF16 = jnp.bfloat16
FORWARD_FIRST = 11
BACKWARD_FIRST = 11
HEAD_FIRST = 4
VMEM_LIMIT = 24 * 1024 * 1024


def rotated(n, first):
    return [(first + i) % n for i in range(n)]


def dot(a, b, contract):
    return lax.dot_general(a, b, ((contract[0], contract[1]), ((), ())), preferred_element_type=F32)


def nn(a, b):
    return dot(a, b, ((1,), (0,)))


def nt(a, b):
    return dot(a, b, ((1,), (1,)))


def tn(a, b):
    return dot(a, b, ((0,), (0,)))


def head_columns(h):
    return slice(h * HD, (h + 1) * HD)


def call(kernel, out_shape, *operands, **extra):
    return pl.pallas_call(
        kernel,
        out_shape=out_shape,
        compiler_params=pltpu.CompilerParams(vmem_limit_bytes=VMEM_LIMIT),
        **extra,
    )(*operands)


def shape_of(shape, dtype=F32):
    return jax.ShapeDtypeStruct(shape, dtype)


def state_of_heads(ref, heads):
    return ref[...].reshape(heads, HD, HD).astype(BF16)


def store_state(state_ref, heads, h, state):
    per_head = state_ref.shape[0] // heads
    state_ref[h * per_head : (h + 1) * per_head] = state.reshape(per_head, state_ref.shape[1], HD)


def outer_kernel(heads, a_hbm, b_hbm, state_ref, a_ref, b_ref, sems):
    copies = []
    parts = halves(a_ref.shape[0])
    for j, rows in enumerate(parts):
        pair = []
        for i, (source, target) in enumerate(((a_hbm, a_ref), (b_hbm, b_ref))):
            copy = pltpu.make_async_copy(source.at[rows], target.at[rows], sems.at[j, i])
            copy.start()
            pair.append(copy)
        copies.append(pair)
    states = [None] * heads
    for j, rows in enumerate(parts):
        for copy in copies[j]:
            copy.wait()
        for h in range(heads):
            cols = head_columns(h)
            state = tn(a_ref[rows, cols], b_ref[rows, cols])
            states[h] = state if j == 0 else states[h] + state
    for h in range(heads):
        store_state(state_ref, heads, h, states[h])


def scan_kernel(slots, part_ref, out_ref):
    total = jnp.zeros(part_ref.shape[1:], F32)
    for slot in slots:
        out_ref[slot] = total
        if slot != slots[-1]:
            total = total + part_ref[slot]


def causal_mask(rows):
    t = lax.broadcasted_iota(jnp.int32, (rows, rows), 0)
    s = lax.broadcasted_iota(jnp.int32, (rows, rows), 1)
    return t >= s


def cut(block, mask):
    return jnp.where(mask, block, 0.0).astype(BF16)


def halves(tokens):
    return slice(0, tokens // 2), slice(tokens // 2, tokens)


def attend_kernel(heads, q_ref, k_ref, v_ref, p_ref, c_ref, g_ref, a_ref, w_ref, sums_ref):
    tokens = q_ref.shape[0]
    state = state_of_heads(p_ref, heads)
    mask = causal_mask(tokens // 2)
    first, second = halves(tokens)
    squares = [jnp.zeros((tokens // 2, HD), F32)] * 2
    inner = [jnp.zeros((tokens // 2, HD), F32)] * 2
    for h in range(heads):
        cols = head_columns(h)
        q0, q1 = q_ref[first, cols], q_ref[second, cols]
        k0, k1 = k_ref[first, cols], k_ref[second, cols]
        w00 = cut(nt(q0, k0), mask)
        w10 = nt(q1, k0).astype(BF16)
        w11 = cut(nt(q1, k1), mask)
        w_ref[h, 0] = w00
        w_ref[h, 1] = w10
        w_ref[h, 2] = w11
    for h in range(heads):
        cols = head_columns(h)
        q0, q1 = q_ref[first, cols], q_ref[second, cols]
        v0, v1 = v_ref[first, cols], v_ref[second, cols]
        w00, w10, w11 = w_ref[h, 0], w_ref[h, 1], w_ref[h, 2]
        attended = (
            nn(q0, state[h]) + nn(w00, v0),
            nn(q1, state[h]) + (nn(w10, v0) + nn(w11, v1)),
        )
        for i, rows in enumerate((first, second)):
            a_ref[rows, cols] = attended[i]
    for h in range(heads):
        cols = head_columns(h)
        for i, rows in enumerate((first, second)):
            part = a_ref[rows, cols]
            scaled = c_ref[rows, cols].astype(F32) * g_ref[:, cols]
            squares[i] = squares[i] + part * part
            inner[i] = inner[i] + scaled * part
    squares = jnp.concatenate([jnp.sum(part.T, axis=0, keepdims=True) for part in squares], axis=1)
    inner = jnp.concatenate([jnp.sum(part.T, axis=0, keepdims=True) for part in inner], axis=1)
    both = jnp.concatenate([squares, inner], axis=0)
    for i in range(sums_ref.shape[0]):
        sums_ref[i] = both


def norm_columns(s_ref):
    sums = s_ref[0]
    for i in range(1, s_ref.shape[0]):
        sums = sums + s_ref[i]
    inverse = lax.rsqrt(sums[0:1] / FEAT + EPS)
    slope = sums[1:2] * inverse * inverse / FEAT
    tokens = sums.shape[1]
    rows = jnp.concatenate(
        [jnp.broadcast_to(inverse, (64, tokens)), jnp.broadcast_to(slope, (64, tokens))], axis=0
    ).T
    return rows[:, 0:1], rows[:, 64:65]


def norm_kernel(heads, s_ref, a_ref, c_ref, g_ref, q_ref, d_ref, state_ref, o_ref):
    inverse, slope = norm_columns(s_ref)
    for h in range(heads):
        cols = head_columns(h)
        scaled = c_ref[:, cols].astype(F32) * g_ref[:, cols]
        grad = (inverse * (scaled - a_ref[:, cols] * slope)).astype(BF16)
        d_ref[:, cols] = grad
        store_state(state_ref, heads, h, tn(q_ref[:, cols], grad))
        o_ref[:, cols] = (a_ref[:, cols] * inverse * g_ref[:, cols]).astype(BF16)


def grad_kernel(
    heads, r_ref, d_ref, q_ref, k_ref, v_ref, w_ref, p_ref, o_ref,
    o_hbm, gq_hbm, gk_hbm, gv_hbm, gq_ref, gk_ref, gv_ref, gw_ref, sems,
):
    copies = []

    def send(i, h, source, target):
        cols = head_columns(h)
        copy = pltpu.make_async_copy(source.at[:, cols], target.at[:, cols], sems.at[i, h])
        copy.start()
        copies.append(copy)

    for h in range(heads):
        send(0, h, o_ref, o_hbm)
    tokens = q_ref.shape[0]
    first, second = halves(tokens)
    mask = causal_mask(tokens // 2)
    prefix = state_of_heads(p_ref, heads)
    suffix = state_of_heads(r_ref, heads)
    for h in range(heads):
        cols = head_columns(h)
        v0, v1 = v_ref[first, cols], v_ref[second, cols]
        d0, d1 = d_ref[first, cols], d_ref[second, cols]
        gw_ref[h, 0] = cut(nt(d0, v0), mask)
        gw_ref[h, 1] = nt(d1, v0).astype(BF16)
        gw_ref[h, 2] = cut(nt(d1, v1), mask)
    for h in range(heads):
        cols = head_columns(h)
        q0, q1 = q_ref[first, cols], q_ref[second, cols]
        k0, k1 = k_ref[first, cols], k_ref[second, cols]
        v0, v1 = v_ref[first, cols], v_ref[second, cols]
        d0, d1 = d_ref[first, cols], d_ref[second, cols]
        g00, g10, g11 = gw_ref[h, 0], gw_ref[h, 1], gw_ref[h, 2]
        gq_ref[first, cols] = (nt(d0, prefix[h]) + nn(g00, k0)).astype(BF16)
        gq_ref[second, cols] = (nt(d1, prefix[h]) + (nn(g10, k0) + nn(g11, k1))).astype(BF16)
        send(1, h, gq_ref, gq_hbm)
        gk_ref[first, cols] = (nt(v0, suffix[h]) + (tn(g00, q0) + tn(g10, q1))).astype(BF16)
        gk_ref[second, cols] = (nt(v1, suffix[h]) + tn(g11, q1)).astype(BF16)
        send(2, h, gk_ref, gk_hbm)
        w00, w10, w11 = w_ref[h, 0], w_ref[h, 1], w_ref[h, 2]
        gv_ref[first, cols] = (nn(k0, suffix[h]) + (tn(w00, d0) + tn(w10, d1))).astype(BF16)
        gv_ref[second, cols] = (nn(k1, suffix[h]) + tn(w11, d1)).astype(BF16)
        send(3, h, gv_ref, gv_hbm)
    for copy in copies:
        copy.wait()


def exchange(parts, axis, order):
    return lax.all_to_all(parts, axis, 0, 0, tiled=True, axis_index_groups=[order])


def exclusive_scan(local, slots, order):
    pieces = exchange(local, "seq", order)
    sums = call(functools.partial(scan_kernel, slots), shape_of(local.shape), pieces)
    return exchange(sums, "seq", order)


def per_device(queries, key_vectors, value_vectors, norm_gain, cotangent):
    tokens, features = queries.shape
    heads = features // HD
    seq = lax.axis_size("seq")
    head_devices = lax.axis_size("head")
    state_shape = (seq, heads * HD // seq, HD)
    wide = (tokens, features)
    gain = norm_gain.reshape(1, features)

    def bind(kernel):
        return lambda *refs: kernel(heads, *refs)

    in_hbm = pl.BlockSpec(memory_space=pltpu.HBM)
    in_vmem = pl.BlockSpec(memory_space=pltpu.VMEM)

    with jax.named_scope("key_value_state"):
        local_kv = call(
            bind(outer_kernel),
            shape_of(state_shape),
            pltpu.with_memory_space_constraint(key_vectors, pltpu.HBM),
            pltpu.with_memory_space_constraint(value_vectors, pltpu.HBM),
            in_specs=[in_hbm, in_hbm],
            out_specs=in_vmem,
            scratch_shapes=[
                pltpu.VMEM(wide, BF16),
                pltpu.VMEM(wide, BF16),
                pltpu.SemaphoreType.DMA((heads, 2)),
            ],
        )
    with jax.named_scope("prefix"):
        order = rotated(seq, FORWARD_FIRST)
        prefix = exclusive_scan(local_kv, [order.index(m) for m in range(seq)], order)
    with jax.named_scope("attended"):
        attended, weights, sums = call(
            bind(attend_kernel),
            (
                shape_of(wide),
                shape_of((heads, 3, tokens // 2, tokens // 2), BF16),
                shape_of((head_devices, 2, tokens)),
            ),
            queries,
            key_vectors,
            value_vectors,
            prefix,
            cotangent,
            gain,
        )
        sums = exchange(sums, "head", rotated(head_devices, HEAD_FIRST))
    with jax.named_scope("norm"):
        out_grad, local_qg, layer_out = call(
            bind(norm_kernel),
            (shape_of(wide, BF16), shape_of(state_shape), shape_of(wide, BF16)),
            sums,
            attended,
            cotangent,
            gain,
            queries,
        )
    with jax.named_scope("suffix"):
        order = rotated(seq, BACKWARD_FIRST)
        suffix = exclusive_scan(local_qg, [order.index(m) for m in reversed(range(seq))], order)
    with jax.named_scope("grads"):
        return call(
            bind(grad_kernel),
            (shape_of(wide, BF16),) * 4,
            suffix,
            out_grad,
            queries,
            key_vectors,
            value_vectors,
            weights,
            prefix,
            layer_out,
            in_specs=[in_vmem] * 8,
            out_specs=[in_hbm] * 4,
            scratch_shapes=[pltpu.VMEM(wide, BF16)] * 3 + [pltpu.VMEM((heads, 3, tokens // 2, tokens // 2), BF16), pltpu.SemaphoreType.DMA((4, heads))],
        )


def solution(mesh):
    split = P(("dp", "seq"), "head")
    return jax.shard_map(
        per_device,
        mesh=mesh,
        in_specs=(split, split, split, P("head"), split),
        out_specs=(split, split, split, split),
        check_vma=False,
    )
```

```python
import functools

import jax
import jax.numpy as jnp
from jax import lax
from jax.experimental import pallas as pl
from jax.experimental.pallas import tpu as pltpu
from jax.sharding import PartitionSpec as P

HD = 128
FEAT = 4096
EPS = 1e-06
F32 = jnp.float32
BF16 = jnp.bfloat16
FORWARD_FIRST = 15
BACKWARD_FIRST = 10
HEAD_FIRST = 4
VMEM_LIMIT = 24 * 1024 * 1024


def rotated(n, first):
    return [(first + i) % n for i in range(n)]


def dot(a, b, contract):
    return lax.dot_general(a, b, ((contract[0], contract[1]), ((), ())), preferred_element_type=F32)


def nn(a, b):
    return dot(a, b, ((1,), (0,)))


def nt(a, b):
    return dot(a, b, ((1,), (1,)))


def tn(a, b):
    return dot(a, b, ((0,), (0,)))


def head_columns(h):
    return slice(h * HD, (h + 1) * HD)


def call(kernel, out_shape, *operands, **extra):
    return pl.pallas_call(
        kernel,
        out_shape=out_shape,
        compiler_params=pltpu.CompilerParams(vmem_limit_bytes=VMEM_LIMIT),
        **extra,
    )(*operands)


def shape_of(shape, dtype=F32):
    return jax.ShapeDtypeStruct(shape, dtype)


def state_of_heads(ref, heads):
    return ref[...].reshape(heads, HD, HD).astype(BF16)


def store_state(state_ref, heads, h, state):
    per_head = state_ref.shape[0] // heads
    state_ref[h * per_head : (h + 1) * per_head] = state.reshape(per_head, state_ref.shape[1], HD)


def outer_kernel(heads, a_hbm, b_hbm, state_ref, a_ref, b_ref, sems):
    copies = []
    parts = halves(a_ref.shape[0])
    for j, rows in enumerate(parts):
        pair = []
        for i, (source, target) in enumerate(((a_hbm, a_ref), (b_hbm, b_ref))):
            copy = pltpu.make_async_copy(source.at[rows], target.at[rows], sems.at[j, i])
            copy.start()
            pair.append(copy)
        copies.append(pair)
    states = [None] * heads
    for j, rows in enumerate(parts):
        for copy in copies[j]:
            copy.wait()
        for h in range(heads):
            cols = head_columns(h)
            state = tn(a_ref[rows, cols], b_ref[rows, cols])
            states[h] = state if j == 0 else states[h] + state
    for h in range(heads):
        store_state(state_ref, heads, h, states[h])


def scan_kernel(slots, part_ref, out_ref):
    total = jnp.zeros(part_ref.shape[1:], F32)
    for slot in slots:
        out_ref[slot] = total
        if slot != slots[-1]:
            total = total + part_ref[slot]


def causal_mask(rows):
    t = lax.broadcasted_iota(jnp.int32, (rows, rows), 0)
    s = lax.broadcasted_iota(jnp.int32, (rows, rows), 1)
    return t >= s


def cut(block, mask):
    return jnp.where(mask, block, 0.0).astype(BF16)


def halves(tokens):
    return slice(0, tokens // 2), slice(tokens // 2, tokens)


def attend_kernel(heads, q_ref, k_ref, v_ref, p_ref, c_ref, g_ref, a_ref, w_ref, sums_ref):
    tokens = q_ref.shape[0]
    state = state_of_heads(p_ref, heads)
    mask = causal_mask(tokens // 2)
    first, second = halves(tokens)
    squares = [jnp.zeros((tokens // 2, HD), F32)] * 2
    inner = [jnp.zeros((tokens // 2, HD), F32)] * 2
    for h in range(heads):
        cols = head_columns(h)
        q0, q1 = q_ref[first, cols], q_ref[second, cols]
        k0, k1 = k_ref[first, cols], k_ref[second, cols]
        w00 = cut(nt(q0, k0), mask)
        w10 = nt(q1, k0).astype(BF16)
        w11 = cut(nt(q1, k1), mask)
        w_ref[h, 0] = w00
        w_ref[h, 1] = w10
        w_ref[h, 2] = w11
    for h in range(heads):
        cols = head_columns(h)
        q0, q1 = q_ref[first, cols], q_ref[second, cols]
        v0, v1 = v_ref[first, cols], v_ref[second, cols]
        w00, w10, w11 = w_ref[h, 0], w_ref[h, 1], w_ref[h, 2]
        attended = (
            nn(q0, state[h]) + nn(w00, v0),
            nn(q1, state[h]) + (nn(w10, v0) + nn(w11, v1)),
        )
        for i, rows in enumerate((first, second)):
            a_ref[rows, cols] = attended[i]
    for h in range(heads):
        cols = head_columns(h)
        for i, rows in enumerate((first, second)):
            part = a_ref[rows, cols]
            scaled = c_ref[rows, cols].astype(F32) * g_ref[:, cols]
            squares[i] = squares[i] + part * part
            inner[i] = inner[i] + scaled * part
    squares = jnp.concatenate([jnp.sum(part.T, axis=0, keepdims=True) for part in squares], axis=1)
    inner = jnp.concatenate([jnp.sum(part.T, axis=0, keepdims=True) for part in inner], axis=1)
    both = jnp.concatenate([squares, inner], axis=0)
    for i in range(sums_ref.shape[0]):
        sums_ref[i] = both


def norm_columns(s_ref):
    sums = s_ref[0]
    for i in range(1, s_ref.shape[0]):
        sums = sums + s_ref[i]
    inverse = lax.rsqrt(sums[0:1] / FEAT + EPS)
    slope = sums[1:2] * inverse * inverse / FEAT
    tokens = sums.shape[1]
    rows = jnp.concatenate(
        [jnp.broadcast_to(inverse, (64, tokens)), jnp.broadcast_to(slope, (64, tokens))], axis=0
    ).T
    return rows[:, 0:1], rows[:, 64:65]


def norm_kernel(heads, s_ref, a_ref, c_ref, g_ref, q_ref, d_ref, state_ref, o_ref):
    inverse, slope = norm_columns(s_ref)
    for h in range(heads):
        cols = head_columns(h)
        scaled = c_ref[:, cols].astype(F32) * g_ref[:, cols]
        grad = (inverse * (scaled - a_ref[:, cols] * slope)).astype(BF16)
        d_ref[:, cols] = grad
        store_state(state_ref, heads, h, tn(q_ref[:, cols], grad))
        o_ref[:, cols] = (a_ref[:, cols] * inverse * g_ref[:, cols]).astype(BF16)


def grad_kernel(
    heads, r_ref, d_ref, q_ref, k_ref, v_ref, w_ref, p_ref, o_ref,
    o_hbm, gq_hbm, gk_hbm, gv_hbm, gq_ref, gk_ref, gv_ref, gw_ref, sems,
):
    copies = []

    def send(i, h, source, target):
        cols = head_columns(h)
        copy = pltpu.make_async_copy(source.at[:, cols], target.at[:, cols], sems.at[i, h])
        copy.start()
        copies.append(copy)

    for h in range(heads):
        send(0, h, o_ref, o_hbm)
    tokens = q_ref.shape[0]
    first, second = halves(tokens)
    mask = causal_mask(tokens // 2)
    prefix = state_of_heads(p_ref, heads)
    suffix = state_of_heads(r_ref, heads)
    for h in range(heads):
        cols = head_columns(h)
        v0, v1 = v_ref[first, cols], v_ref[second, cols]
        d0, d1 = d_ref[first, cols], d_ref[second, cols]
        gw_ref[h, 0] = cut(nt(d0, v0), mask)
        gw_ref[h, 1] = nt(d1, v0).astype(BF16)
        gw_ref[h, 2] = cut(nt(d1, v1), mask)
    for h in range(heads):
        cols = head_columns(h)
        q0, q1 = q_ref[first, cols], q_ref[second, cols]
        k0, k1 = k_ref[first, cols], k_ref[second, cols]
        v0, v1 = v_ref[first, cols], v_ref[second, cols]
        d0, d1 = d_ref[first, cols], d_ref[second, cols]
        g00, g10, g11 = gw_ref[h, 0], gw_ref[h, 1], gw_ref[h, 2]
        gq_ref[first, cols] = (nt(d0, prefix[h]) + nn(g00, k0)).astype(BF16)
        gq_ref[second, cols] = (nt(d1, prefix[h]) + (nn(g10, k0) + nn(g11, k1))).astype(BF16)
        send(1, h, gq_ref, gq_hbm)
        gk_ref[first, cols] = (nt(v0, suffix[h]) + (tn(g00, q0) + tn(g10, q1))).astype(BF16)
        gk_ref[second, cols] = (nt(v1, suffix[h]) + tn(g11, q1)).astype(BF16)
        send(2, h, gk_ref, gk_hbm)
        w00, w10, w11 = w_ref[h, 0], w_ref[h, 1], w_ref[h, 2]
        gv_ref[first, cols] = (nn(k0, suffix[h]) + (tn(w00, d0) + tn(w10, d1))).astype(BF16)
        gv_ref[second, cols] = (nn(k1, suffix[h]) + tn(w11, d1)).astype(BF16)
        send(3, h, gv_ref, gv_hbm)
    for copy in copies:
        copy.wait()


def exchange(parts, axis, order):
    return lax.all_to_all(parts, axis, 0, 0, tiled=True, axis_index_groups=[order])


def exclusive_scan(local, slots, order):
    pieces = exchange(local, "seq", order)
    sums = call(functools.partial(scan_kernel, slots), shape_of(local.shape), pieces)
    return exchange(sums, "seq", order)


def per_device(queries, key_vectors, value_vectors, norm_gain, cotangent):
    tokens, features = queries.shape
    heads = features // HD
    seq = lax.axis_size("seq")
    head_devices = lax.axis_size("head")
    state_shape = (seq, heads * HD // seq, HD)
    wide = (tokens, features)
    gain = norm_gain.reshape(1, features)

    def bind(kernel):
        return lambda *refs: kernel(heads, *refs)

    in_hbm = pl.BlockSpec(memory_space=pltpu.HBM)
    in_vmem = pl.BlockSpec(memory_space=pltpu.VMEM)

    with jax.named_scope("key_value_state"):
        local_kv = call(
            bind(outer_kernel),
            shape_of(state_shape),
            pltpu.with_memory_space_constraint(key_vectors, pltpu.HBM),
            pltpu.with_memory_space_constraint(value_vectors, pltpu.HBM),
            in_specs=[in_hbm, in_hbm],
            out_specs=in_vmem,
            scratch_shapes=[
                pltpu.VMEM(wide, BF16),
                pltpu.VMEM(wide, BF16),
                pltpu.SemaphoreType.DMA((heads, 2)),
            ],
        )
    with jax.named_scope("prefix"):
        order = rotated(seq, FORWARD_FIRST)
        prefix = exclusive_scan(local_kv, [order.index(m) for m in range(seq)], order)
    with jax.named_scope("attended"):
        attended, weights, sums = call(
            bind(attend_kernel),
            (
                shape_of(wide),
                shape_of((heads, 3, tokens // 2, tokens // 2), BF16),
                shape_of((head_devices, 2, tokens)),
            ),
            queries,
            key_vectors,
            value_vectors,
            prefix,
            cotangent,
            gain,
        )
        sums = exchange(sums, "head", rotated(head_devices, HEAD_FIRST))
    with jax.named_scope("norm"):
        out_grad, local_qg, layer_out = call(
            bind(norm_kernel),
            (shape_of(wide, BF16), shape_of(state_shape), shape_of(wide, BF16)),
            sums,
            attended,
            cotangent,
            gain,
            queries,
        )
    with jax.named_scope("suffix"):
        order = rotated(seq, BACKWARD_FIRST)
        suffix = exclusive_scan(local_qg, [order.index(m) for m in reversed(range(seq))], order)
    with jax.named_scope("grads"):
        return call(
            bind(grad_kernel),
            (shape_of(wide, BF16),) * 4,
            suffix,
            out_grad,
            queries,
            key_vectors,
            value_vectors,
            weights,
            prefix,
            layer_out,
            in_specs=[in_vmem] * 8,
            out_specs=[in_hbm] * 4,
            scratch_shapes=[pltpu.VMEM(wide, BF16)] * 3 + [pltpu.VMEM((heads, 3, tokens // 2, tokens // 2), BF16), pltpu.SemaphoreType.DMA((4, heads))],
        )


def solution(mesh):
    split = P(("dp", "seq"), "head")
    return jax.shard_map(
        per_device,
        mesh=mesh,
        in_specs=(split, split, split, P("head"), split),
        out_specs=(split, split, split, split),
        check_vma=False,
    )
```

```python
import functools

import jax
import jax.numpy as jnp
from jax import lax
from jax.experimental import pallas as pl
from jax.experimental.pallas import tpu as pltpu
from jax.sharding import PartitionSpec as P

HD = 128
FEAT = 4096
EPS = 1e-06
F32 = jnp.float32
BF16 = jnp.bfloat16
FORWARD_FIRST = (15, 11)
BACKWARD_FIRST = (10, 10)
HEAD_FIRST = 4
VMEM_LIMIT = 24 * 1024 * 1024


def rotated(n, first):
    return [(first + i) % n for i in range(n)]


def dot(a, b, contract):
    return lax.dot_general(a, b, ((contract[0], contract[1]), ((), ())), preferred_element_type=F32)


def nn(a, b):
    return dot(a, b, ((1,), (0,)))


def nt(a, b):
    return dot(a, b, ((1,), (1,)))


def tn(a, b):
    return dot(a, b, ((0,), (0,)))


def head_columns(h):
    return slice(h * HD, (h + 1) * HD)


def call(kernel, out_shape, *operands, **extra):
    return pl.pallas_call(
        kernel,
        out_shape=out_shape,
        compiler_params=pltpu.CompilerParams(vmem_limit_bytes=VMEM_LIMIT),
        **extra,
    )(*operands)


def shape_of(shape, dtype=F32):
    return jax.ShapeDtypeStruct(shape, dtype)


def state_of_heads(ref, slots, heads):
    chunks = jnp.concatenate([ref[slot] for slot in slots], axis=0)
    return chunks.reshape(heads, HD, HD).astype(BF16)


def store_state(state_ref, heads, h, state):
    per_head = state_ref.shape[0] // heads
    state_ref[h * per_head : (h + 1) * per_head] = state.reshape(per_head, state_ref.shape[1], HD)


def outer_kernel(heads, a_hbm, b_hbm, state_ref, a_ref, b_ref, sems):
    copies = []
    parts = halves(a_ref.shape[0])
    for j, rows in enumerate(parts):
        pair = []
        for i, (source, target) in enumerate(((a_hbm, a_ref), (b_hbm, b_ref))):
            copy = pltpu.make_async_copy(source.at[rows], target.at[rows], sems.at[j, i])
            copy.start()
            pair.append(copy)
        copies.append(pair)
    states = [None] * heads
    for j, rows in enumerate(parts):
        for copy in copies[j]:
            copy.wait()
        for h in range(heads):
            cols = head_columns(h)
            state = tn(a_ref[rows, cols], b_ref[rows, cols])
            states[h] = state if j == 0 else states[h] + state
    for h in range(heads):
        store_state(state_ref, heads, h, states[h])


def scan_kernel(devices, there, back, part_ref, out_ref):
    total = jnp.zeros(part_ref.shape[1:], F32)
    for device in devices:
        out_ref[back.index(device)] = total
        if device != devices[-1]:
            total = total + part_ref[there.index(device)]


def causal_mask(rows):
    t = lax.broadcasted_iota(jnp.int32, (rows, rows), 0)
    s = lax.broadcasted_iota(jnp.int32, (rows, rows), 1)
    return t >= s


def cut(block, mask):
    return jnp.where(mask, block, 0.0).astype(BF16)


def halves(tokens):
    return slice(0, tokens // 2), slice(tokens // 2, tokens)


def attend_kernel(prefix_slots, heads, q_ref, k_ref, v_ref, p_ref, c_ref, g_ref, a_ref, w_ref, sums_ref):
    tokens = q_ref.shape[0]
    state = state_of_heads(p_ref, prefix_slots, heads)
    mask = causal_mask(tokens // 2)
    first, second = halves(tokens)
    squares = [jnp.zeros((tokens // 2, HD), F32)] * 2
    inner = [jnp.zeros((tokens // 2, HD), F32)] * 2
    for h in range(heads):
        cols = head_columns(h)
        q0, q1 = q_ref[first, cols], q_ref[second, cols]
        k0, k1 = k_ref[first, cols], k_ref[second, cols]
        w00 = cut(nt(q0, k0), mask)
        w10 = nt(q1, k0).astype(BF16)
        w11 = cut(nt(q1, k1), mask)
        w_ref[h, 0] = w00
        w_ref[h, 1] = w10
        w_ref[h, 2] = w11
    for h in range(heads):
        cols = head_columns(h)
        q0, q1 = q_ref[first, cols], q_ref[second, cols]
        v0, v1 = v_ref[first, cols], v_ref[second, cols]
        w00, w10, w11 = w_ref[h, 0], w_ref[h, 1], w_ref[h, 2]
        attended = (
            nn(q0, state[h]) + nn(w00, v0),
            nn(q1, state[h]) + (nn(w10, v0) + nn(w11, v1)),
        )
        for i, rows in enumerate((first, second)):
            a_ref[rows, cols] = attended[i]
            scaled = c_ref[rows, cols].astype(F32) * g_ref[:, cols]
            squares[i] = squares[i] + attended[i] * attended[i]
            inner[i] = inner[i] + scaled * attended[i]
    squares = jnp.concatenate([jnp.sum(part.T, axis=0, keepdims=True) for part in squares], axis=1)
    inner = jnp.concatenate([jnp.sum(part.T, axis=0, keepdims=True) for part in inner], axis=1)
    both = jnp.concatenate([squares, inner], axis=0)
    for i in range(sums_ref.shape[0]):
        sums_ref[i] = both


def norm_columns(s_ref):
    sums = s_ref[0]
    for i in range(1, s_ref.shape[0]):
        sums = sums + s_ref[i]
    inverse = lax.rsqrt(sums[0:1] / FEAT + EPS)
    slope = sums[1:2] * inverse * inverse / FEAT
    tokens = sums.shape[1]
    rows = jnp.concatenate(
        [jnp.broadcast_to(inverse, (64, tokens)), jnp.broadcast_to(slope, (64, tokens))], axis=0
    ).T
    return rows[:, 0:1], rows[:, 64:65]


def norm_kernel(heads, s_ref, a_ref, c_ref, g_ref, q_ref, d_ref, state_ref, o_ref):
    inverse, slope = norm_columns(s_ref)
    for h in range(heads):
        cols = head_columns(h)
        scaled = c_ref[:, cols].astype(F32) * g_ref[:, cols]
        grad = (inverse * (scaled - a_ref[:, cols] * slope)).astype(BF16)
        d_ref[:, cols] = grad
        store_state(state_ref, heads, h, tn(q_ref[:, cols], grad))
        o_ref[:, cols] = (a_ref[:, cols] * inverse * g_ref[:, cols]).astype(BF16)


def grad_kernel(
    prefix_slots, suffix_slots, heads, r_ref, d_ref, q_ref, k_ref, v_ref, w_ref, p_ref, o_ref,
    o_hbm, gq_hbm, gk_hbm, gv_hbm, gq_ref, gk_ref, gv_ref, gw_ref, sems,
):
    copies = []

    def send(i, h, source, target):
        cols = head_columns(h)
        copy = pltpu.make_async_copy(source.at[:, cols], target.at[:, cols], sems.at[i, h])
        copy.start()
        copies.append(copy)

    for h in range(heads):
        send(0, h, o_ref, o_hbm)
    tokens = q_ref.shape[0]
    first, second = halves(tokens)
    mask = causal_mask(tokens // 2)
    prefix = state_of_heads(p_ref, prefix_slots, heads)
    suffix = state_of_heads(r_ref, suffix_slots, heads)
    for h in range(heads):
        cols = head_columns(h)
        v0, v1 = v_ref[first, cols], v_ref[second, cols]
        d0, d1 = d_ref[first, cols], d_ref[second, cols]
        gw_ref[h, 0] = cut(nt(d0, v0), mask)
        gw_ref[h, 1] = nt(d1, v0).astype(BF16)
        gw_ref[h, 2] = cut(nt(d1, v1), mask)
    for h in range(heads):
        cols = head_columns(h)
        q0, q1 = q_ref[first, cols], q_ref[second, cols]
        k0, k1 = k_ref[first, cols], k_ref[second, cols]
        v0, v1 = v_ref[first, cols], v_ref[second, cols]
        d0, d1 = d_ref[first, cols], d_ref[second, cols]
        g00, g10, g11 = gw_ref[h, 0], gw_ref[h, 1], gw_ref[h, 2]
        gq_ref[first, cols] = (nt(d0, prefix[h]) + nn(g00, k0)).astype(BF16)
        gq_ref[second, cols] = (nt(d1, prefix[h]) + (nn(g10, k0) + nn(g11, k1))).astype(BF16)
        send(1, h, gq_ref, gq_hbm)
        gk_ref[first, cols] = (nt(v0, suffix[h]) + (tn(g00, q0) + tn(g10, q1))).astype(BF16)
        gk_ref[second, cols] = (nt(v1, suffix[h]) + tn(g11, q1)).astype(BF16)
        send(2, h, gk_ref, gk_hbm)
        w00, w10, w11 = w_ref[h, 0], w_ref[h, 1], w_ref[h, 2]
        gv_ref[first, cols] = (nn(k0, suffix[h]) + (tn(w00, d0) + tn(w10, d1))).astype(BF16)
        gv_ref[second, cols] = (nn(k1, suffix[h]) + tn(w11, d1)).astype(BF16)
        send(3, h, gv_ref, gv_hbm)
    for copy in copies:
        copy.wait()


def exchange(parts, axis, order):
    return lax.all_to_all(parts, axis, 0, 0, tiled=True, axis_index_groups=[order])


def exclusive_scan(local, devices, there, back):
    pieces = exchange(local, "seq", there)
    kernel = functools.partial(scan_kernel, devices, there, back)
    sums = call(kernel, shape_of(local.shape), pieces)
    return exchange(sums, "seq", back), [back.index(device) for device in there]


def per_device(queries, key_vectors, value_vectors, norm_gain, cotangent):
    tokens, features = queries.shape
    heads = features // HD
    seq = lax.axis_size("seq")
    head_devices = lax.axis_size("head")
    state_shape = (seq, heads * HD // seq, HD)
    wide = (tokens, features)
    gain = norm_gain.reshape(1, features)

    def bind(kernel):
        return lambda *refs: kernel(heads, *refs)

    in_hbm = pl.BlockSpec(memory_space=pltpu.HBM)
    in_vmem = pl.BlockSpec(memory_space=pltpu.VMEM)

    with jax.named_scope("key_value_state"):
        local_kv = call(
            bind(outer_kernel),
            shape_of(state_shape),
            pltpu.with_memory_space_constraint(key_vectors, pltpu.HBM),
            pltpu.with_memory_space_constraint(value_vectors, pltpu.HBM),
            in_specs=[in_hbm, in_hbm],
            out_specs=in_vmem,
            scratch_shapes=[
                pltpu.VMEM(wide, BF16),
                pltpu.VMEM(wide, BF16),
                pltpu.SemaphoreType.DMA((heads, 2)),
            ],
        )
    with jax.named_scope("prefix"):
        there, back = (rotated(seq, first) for first in FORWARD_FIRST)
        prefix, prefix_slots = exclusive_scan(local_kv, list(range(seq)), there, back)
    with jax.named_scope("attended"):
        attended, weights, sums = call(
            bind(functools.partial(attend_kernel, prefix_slots)),
            (
                shape_of(wide),
                shape_of((heads, 3, tokens // 2, tokens // 2), BF16),
                shape_of((head_devices, 2, tokens)),
            ),
            queries,
            key_vectors,
            value_vectors,
            prefix,
            cotangent,
            gain,
        )
        sums = exchange(sums, "head", rotated(head_devices, HEAD_FIRST))
    with jax.named_scope("norm"):
        out_grad, local_qg, layer_out = call(
            bind(norm_kernel),
            (shape_of(wide, BF16), shape_of(state_shape), shape_of(wide, BF16)),
            sums,
            attended,
            cotangent,
            gain,
            queries,
        )
    with jax.named_scope("suffix"):
        there, back = (rotated(seq, first) for first in BACKWARD_FIRST)
        suffix, suffix_slots = exclusive_scan(local_qg, list(range(seq))[::-1], there, back)
    with jax.named_scope("grads"):
        return call(
            bind(functools.partial(grad_kernel, prefix_slots, suffix_slots)),
            (shape_of(wide, BF16),) * 4,
            suffix,
            out_grad,
            queries,
            key_vectors,
            value_vectors,
            weights,
            prefix,
            layer_out,
            in_specs=[in_vmem] * 8,
            out_specs=[in_hbm] * 4,
            scratch_shapes=[pltpu.VMEM(wide, BF16)] * 3 + [pltpu.VMEM((heads, 3, tokens // 2, tokens // 2), BF16), pltpu.SemaphoreType.DMA((4, heads))],
        )


def solution(mesh):
    split = P(("dp", "seq"), "head")
    return jax.shard_map(
        per_device,
        mesh=mesh,
        in_specs=(split, split, split, P("head"), split),
        out_specs=(split, split, split, split),
        check_vma=False,
    )
```

```python
import functools

import jax
import jax.numpy as jnp
from jax import lax
from jax.experimental import pallas as pl
from jax.experimental.pallas import tpu as pltpu
from jax.sharding import PartitionSpec as P

HD = 128
FEAT = 4096
EPS = 1e-06
F32 = jnp.float32
BF16 = jnp.bfloat16
FORWARD_FIRST = (15, 11)
BACKWARD_FIRST = (10, 10)
HEAD_FIRST = 5
VMEM_LIMIT = 24 * 1024 * 1024


def rotated(n, first):
    return [(first + i) % n for i in range(n)]


def dot(a, b, contract):
    return lax.dot_general(a, b, ((contract[0], contract[1]), ((), ())), preferred_element_type=F32)


def nn(a, b):
    return dot(a, b, ((1,), (0,)))


def nt(a, b):
    return dot(a, b, ((1,), (1,)))


def tn(a, b):
    return dot(a, b, ((0,), (0,)))


def head_columns(h):
    return slice(h * HD, (h + 1) * HD)


def call(kernel, out_shape, *operands, **extra):
    return pl.pallas_call(
        kernel,
        out_shape=out_shape,
        compiler_params=pltpu.CompilerParams(vmem_limit_bytes=VMEM_LIMIT),
        **extra,
    )(*operands)


def shape_of(shape, dtype=F32):
    return jax.ShapeDtypeStruct(shape, dtype)


def state_of_heads(ref, slots, heads):
    chunks = jnp.concatenate([ref[slot] for slot in slots], axis=0)
    return chunks.reshape(heads, HD, HD).astype(BF16)


def store_state(state_ref, heads, h, state):
    per_head = state_ref.shape[0] // heads
    state_ref[h * per_head : (h + 1) * per_head] = state.reshape(per_head, state_ref.shape[1], HD)


def outer_kernel(heads, a_hbm, b_hbm, state_ref, a_ref, b_ref, sems):
    copies = []
    parts = halves(a_ref.shape[0])
    for j, rows in enumerate(parts):
        pair = []
        for i, (source, target) in enumerate(((a_hbm, a_ref), (b_hbm, b_ref))):
            copy = pltpu.make_async_copy(source.at[rows], target.at[rows], sems.at[j, i])
            copy.start()
            pair.append(copy)
        copies.append(pair)
    states = [None] * heads
    for j, rows in enumerate(parts):
        for copy in copies[j]:
            copy.wait()
        for h in range(heads):
            cols = head_columns(h)
            state = tn(a_ref[rows, cols], b_ref[rows, cols])
            states[h] = state if j == 0 else states[h] + state
    for h in range(heads):
        store_state(state_ref, heads, h, states[h])


def scan_kernel(devices, there, back, part_ref, out_ref):
    total = jnp.zeros(part_ref.shape[1:], F32)
    for device in devices:
        out_ref[back.index(device)] = total
        if device != devices[-1]:
            total = total + part_ref[there.index(device)]


def causal_mask(rows):
    t = lax.broadcasted_iota(jnp.int32, (rows, rows), 0)
    s = lax.broadcasted_iota(jnp.int32, (rows, rows), 1)
    return t >= s


def cut(block, mask):
    return jnp.where(mask, block, 0.0).astype(BF16)


def halves(tokens):
    return slice(0, tokens // 2), slice(tokens // 2, tokens)


def attend_kernel(prefix_slots, heads, q_ref, k_ref, v_ref, p_ref, c_ref, g_ref, a_ref, wt_ref, sums_ref, w_ref):
    tokens = q_ref.shape[0]
    state = state_of_heads(p_ref, prefix_slots, heads)
    mask = causal_mask(tokens // 2)
    first, second = halves(tokens)
    squares = [jnp.zeros((tokens // 2, HD), F32)] * 2
    inner = [jnp.zeros((tokens // 2, HD), F32)] * 2
    for h in range(heads):
        cols = head_columns(h)
        q0, q1 = q_ref[first, cols], q_ref[second, cols]
        k0, k1 = k_ref[first, cols], k_ref[second, cols]
        w00 = cut(nt(q0, k0), mask)
        w10 = nt(q1, k0).astype(BF16)
        w11 = cut(nt(q1, k1), mask)
        w_ref[h, 0] = w00
        w_ref[h, 1] = w10
        w_ref[h, 2] = w11
        wt_ref[h, 0] = w00.T
        wt_ref[h, 1] = w10.T
        wt_ref[h, 2] = w11.T
    for h in range(heads):
        cols = head_columns(h)
        q0, q1 = q_ref[first, cols], q_ref[second, cols]
        v0, v1 = v_ref[first, cols], v_ref[second, cols]
        w00, w10, w11 = w_ref[h, 0], w_ref[h, 1], w_ref[h, 2]
        attended = (
            nn(q0, state[h]) + nn(w00, v0),
            nn(q1, state[h]) + (nn(w10, v0) + nn(w11, v1)),
        )
        for i, rows in enumerate((first, second)):
            a_ref[rows, cols] = attended[i]
            scaled = c_ref[rows, cols].astype(F32) * g_ref[:, cols]
            squares[i] = squares[i] + attended[i] * attended[i]
            inner[i] = inner[i] + scaled * attended[i]
    squares = jnp.concatenate([jnp.sum(part.T, axis=0, keepdims=True) for part in squares], axis=1)
    inner = jnp.concatenate([jnp.sum(part.T, axis=0, keepdims=True) for part in inner], axis=1)
    both = jnp.concatenate([squares, inner], axis=0)
    for i in range(sums_ref.shape[0]):
        sums_ref[i] = both


def norm_columns(s_ref):
    sums = s_ref[0]
    for i in range(1, s_ref.shape[0]):
        sums = sums + s_ref[i]
    inverse = lax.rsqrt(sums[0:1] / FEAT + EPS)
    slope = sums[1:2] * inverse * inverse / FEAT
    tokens = sums.shape[1]
    rows = jnp.concatenate(
        [jnp.broadcast_to(inverse, (64, tokens)), jnp.broadcast_to(slope, (64, tokens))], axis=0
    ).T
    return rows[:, 0:1], rows[:, 64:65]


def norm_kernel(heads, s_ref, a_ref, c_ref, g_ref, q_ref, d_ref, state_ref, o_ref):
    inverse, slope = norm_columns(s_ref)
    for h in range(heads):
        cols = head_columns(h)
        scaled = c_ref[:, cols].astype(F32) * g_ref[:, cols]
        grad = (inverse * (scaled - a_ref[:, cols] * slope)).astype(BF16)
        d_ref[:, cols] = grad
        store_state(state_ref, heads, h, tn(q_ref[:, cols], grad))
        o_ref[:, cols] = (a_ref[:, cols] * inverse * g_ref[:, cols]).astype(BF16)


def grad_kernel(
    prefix_slots, suffix_slots, heads, r_ref, d_ref, q_ref, k_ref, v_ref, w_ref, p_ref, o_ref,
    o_hbm, gq_hbm, gk_hbm, gv_hbm, gq_ref, gk_ref, gv_ref, gw_ref, sems,
):
    copies = []

    def send(i, h, source, target):
        cols = head_columns(h)
        copy = pltpu.make_async_copy(source.at[:, cols], target.at[:, cols], sems.at[i, h])
        copy.start()
        copies.append(copy)

    for h in range(heads):
        send(0, h, o_ref, o_hbm)
    tokens = q_ref.shape[0]
    first, second = halves(tokens)
    mask = causal_mask(tokens // 2)
    prefix = state_of_heads(p_ref, prefix_slots, heads)
    suffix = state_of_heads(r_ref, suffix_slots, heads)
    for h in range(heads):
        cols = head_columns(h)
        v0, v1 = v_ref[first, cols], v_ref[second, cols]
        d0, d1 = d_ref[first, cols], d_ref[second, cols]
        gw_ref[h, 0] = cut(nt(d0, v0), mask)
        gw_ref[h, 1] = nt(d1, v0).astype(BF16)
        gw_ref[h, 2] = cut(nt(d1, v1), mask)
    for h in range(heads):
        cols = head_columns(h)
        q0, q1 = q_ref[first, cols], q_ref[second, cols]
        k0, k1 = k_ref[first, cols], k_ref[second, cols]
        v0, v1 = v_ref[first, cols], v_ref[second, cols]
        d0, d1 = d_ref[first, cols], d_ref[second, cols]
        g00, g10, g11 = gw_ref[h, 0], gw_ref[h, 1], gw_ref[h, 2]
        gq_ref[first, cols] = (nt(d0, prefix[h]) + nn(g00, k0)).astype(BF16)
        gq_ref[second, cols] = (nt(d1, prefix[h]) + (nn(g10, k0) + nn(g11, k1))).astype(BF16)
        send(1, h, gq_ref, gq_hbm)
        gk_ref[first, cols] = (nt(v0, suffix[h]) + (tn(g00, q0) + tn(g10, q1))).astype(BF16)
        gk_ref[second, cols] = (nt(v1, suffix[h]) + tn(g11, q1)).astype(BF16)
        send(2, h, gk_ref, gk_hbm)
        w00, w10, w11 = w_ref[h, 0], w_ref[h, 1], w_ref[h, 2]
        gv_ref[first, cols] = (nn(k0, suffix[h]) + (nn(w00, d0) + nn(w10, d1))).astype(BF16)
        gv_ref[second, cols] = (nn(k1, suffix[h]) + nn(w11, d1)).astype(BF16)
        send(3, h, gv_ref, gv_hbm)
    for copy in copies:
        copy.wait()


def exchange(parts, axis, order):
    return lax.all_to_all(parts, axis, 0, 0, tiled=True, axis_index_groups=[order])


def exclusive_scan(local, devices, there, back):
    pieces = exchange(local, "seq", there)
    kernel = functools.partial(scan_kernel, devices, there, back)
    sums = call(kernel, shape_of(local.shape), pieces)
    return exchange(sums, "seq", back), [back.index(device) for device in there]


def per_device(queries, key_vectors, value_vectors, norm_gain, cotangent):
    tokens, features = queries.shape
    heads = features // HD
    seq = lax.axis_size("seq")
    head_devices = lax.axis_size("head")
    state_shape = (seq, heads * HD // seq, HD)
    wide = (tokens, features)
    gain = norm_gain.reshape(1, features)

    def bind(kernel):
        return lambda *refs: kernel(heads, *refs)

    in_hbm = pl.BlockSpec(memory_space=pltpu.HBM)
    in_vmem = pl.BlockSpec(memory_space=pltpu.VMEM)

    with jax.named_scope("key_value_state"):
        local_kv = call(
            bind(outer_kernel),
            shape_of(state_shape),
            pltpu.with_memory_space_constraint(key_vectors, pltpu.HBM),
            pltpu.with_memory_space_constraint(value_vectors, pltpu.HBM),
            in_specs=[in_hbm, in_hbm],
            out_specs=in_vmem,
            scratch_shapes=[
                pltpu.VMEM(wide, BF16),
                pltpu.VMEM(wide, BF16),
                pltpu.SemaphoreType.DMA((heads, 2)),
            ],
        )
    with jax.named_scope("prefix"):
        there, back = (rotated(seq, first) for first in FORWARD_FIRST)
        prefix, prefix_slots = exclusive_scan(local_kv, list(range(seq)), there, back)
    with jax.named_scope("attended"):
        attended, weights, sums = call(
            bind(functools.partial(attend_kernel, prefix_slots)),
            (
                shape_of(wide),
                shape_of((heads, 3, tokens // 2, tokens // 2), BF16),
                shape_of((head_devices, 2, tokens)),
            ),
            queries,
            key_vectors,
            value_vectors,
            prefix,
            cotangent,
            gain,
            scratch_shapes=[pltpu.VMEM((heads, 3, tokens // 2, tokens // 2), BF16)],
        )
        sums = exchange(sums, "head", rotated(head_devices, HEAD_FIRST))
    with jax.named_scope("norm"):
        out_grad, local_qg, layer_out = call(
            bind(norm_kernel),
            (shape_of(wide, BF16), shape_of(state_shape), shape_of(wide, BF16)),
            sums,
            attended,
            cotangent,
            gain,
            queries,
        )
    with jax.named_scope("suffix"):
        there, back = (rotated(seq, first) for first in BACKWARD_FIRST)
        suffix, suffix_slots = exclusive_scan(local_qg, list(range(seq))[::-1], there, back)
    with jax.named_scope("grads"):
        return call(
            bind(functools.partial(grad_kernel, prefix_slots, suffix_slots)),
            (shape_of(wide, BF16),) * 4,
            suffix,
            out_grad,
            queries,
            key_vectors,
            value_vectors,
            weights,
            prefix,
            layer_out,
            in_specs=[in_vmem] * 8,
            out_specs=[in_hbm] * 4,
            scratch_shapes=[pltpu.VMEM(wide, BF16)] * 3 + [pltpu.VMEM((heads, 3, tokens // 2, tokens // 2), BF16), pltpu.SemaphoreType.DMA((4, heads))],
        )


def solution(mesh):
    split = P(("dp", "seq"), "head")
    return jax.shard_map(
        per_device,
        mesh=mesh,
        in_specs=(split, split, split, P("head"), split),
        out_specs=(split, split, split, split),
        check_vma=False,
    )
```
